32 devices in a mesh: row: 4 (over x, core), col: 4 (over z), depth: 2 (over y).
Axes of the slice: x: 2, y: 2, z: 4, core: 2. Of those that a mesh axis runs over, the one named last changes fastest.
Arguments:
- a_blocks: float32 [128, 8, 64, 128], P(('row', 'col', 'depth')), may hold values from -0.9 to 0.9
- a_index: int32 [128, 8, 2], P(('row', 'col', 'depth')), may hold values from 0 to 255, as said below
- b_blocks: float32 [2048, 4, 64, 256], P(('row', 'depth'), 'col'), may hold values from -0.9 to 0.9
- b_index: int32 [2048, 4, 4], P(('row', 'depth'), 'col'), may hold values from 0 to 511, as said below
- c_index: int32 [128, 4, 6], P('row', 'col'), may hold values from 0 to 511, as said below
Outputs:
- c_blocks: float32 [128, 4, 64, 384], P(('row', 'depth'), 'col')
The draws below stay inside these ranges and needn't reach their ends.
Inputs may be any that keep to these rules, and one draw needn't show every extreme that they name: The pattern is banded: a_index[i, q, s] differs by at most 1 from (2048 * i // 128) // 8, and is clipped to the slab. The pattern is banded: for the row p of b_blocks, whose block row of B is h = (p % 256) * 8 + p // 256, b_index[p, c, b] differs by at most 2 from h // 4, and is clipped to the column tile. The pattern is banded: c_index[i, c, k] differs by at most 4 from (2048 * i // 128) // 4, and is clipped to the column tile.
All inputs are finite; a program needn't handle non-finite values.
Results may differ from the reference program's by a relative error of at most 0.0003.
Values sent between devices are 32-bit elements; how exact they have to be, the bound alone decides.
No kernel may reach another device: no remote copies, remote signals or barrier semaphores. Data moves between devices by JAX's collectives and lax.ppermute only.
A program may use at most 128 MiB of HBM per device.

```python
import jax
import jax.numpy as jnp
from jax import lax

BLK = 64
NB = 2048
MB = 128
KS = 2
KB = 4
KC = 6
NSLAB = 8
SLAB = 256
CW = 512
N_COL = 4
N_DEPTH = 2


def draw_a_index(key, part):
    rows = jnp.arange(MB, dtype=jnp.int32)
    center = rows * NB // MB
    base = center // NSLAB
    step = jax.random.randint(key, (MB, NSLAB, KS), -1, 2, dtype=jnp.int32)
    return jnp.clip(base[:, None, None] + step, 0, SLAB - 1).astype(jnp.int32)


def draw_b_index(key, part):
    place = jnp.arange(NB, dtype=jnp.int32)
    global_row = place % SLAB * NSLAB + place // SLAB
    base = global_row // N_COL
    step = jax.random.randint(key, (NB, N_COL, KB), -N_DEPTH, N_DEPTH + 1, dtype=jnp.int32)
    return jnp.clip(base[:, None, None] + step, 0, CW - 1).astype(jnp.int32)


def draw_c_index(key, part):
    rows = jnp.arange(MB, dtype=jnp.int32)
    center = rows * NB // MB
    base = center // N_COL
    step = jax.random.randint(key, (MB, N_COL, KC), -2 * N_DEPTH, 2 * N_DEPTH + 1, dtype=jnp.int32)
    return jnp.clip(base[:, None, None] + step, 0, CW - 1).astype(jnp.int32)


def shard_levels(own_key, dims, pieces, least, largest):
    def one(position, blocks):
        steps = jax.random.uniform(jax.random.fold_in(jax.random.fold_in(own_key, 6), position), (blocks,), jnp.float32, least / len(pieces), largest / len(pieces))
        return jnp.repeat(jnp.exp(steps), dims[position] // blocks).reshape((-1,) + (1,) * (len(dims) - position - 1))

    factor_of = one(*pieces[0])
    for cut in pieces[1:]:
        factor_of = factor_of * one(*cut)
    return factor_of


def scatter_about(stream_key, shape, scale, bound, shards=(), held_as=jnp.bfloat16):
    level = shard_levels(stream_key, shape, shards, -0.22, 0.18) if shards else 1.0
    drawn = jax.random.normal(stream_key, shape, jnp.float32) * scale * level
    return jnp.minimum(jnp.maximum(drawn, -bound), bound).astype(held_as)


def setup_inputs(seed: int = 0) -> dict:
    key_of = jax.random.split(jax.random.key(seed), 6)
    a_blocks = scatter_about(key_of[0], (MB, NSLAB, BLK, KS * BLK), 0.15, 0.9, ((0, 32),), jnp.float32)
    a_index = draw_a_index(jax.random.fold_in(key_of[5], 71), 0)
    b_blocks = scatter_about(key_of[2], (NB, N_COL, BLK, KB * BLK), 0.15, 0.9, ((0, 8), (1, 4)), jnp.float32)
    b_index = draw_b_index(jax.random.fold_in(key_of[5], 71), 0)
    c_index = draw_c_index(jax.random.fold_in(key_of[5], 71), 0)
    return {"a_blocks": a_blocks, "a_index": a_index, "b_blocks": b_blocks, "b_index": b_index, "c_index": c_index}


def reference(a_blocks, a_index, b_blocks, b_index, c_index):
    def visit(total, slab_index):
        a_vals = lax.dynamic_index_in_dim(a_blocks, slab_index, 1, keepdims=False)
        a_slots = lax.dynamic_index_in_dim(a_index, slab_index, 1, keepdims=False)
        partner = (slab_index * SLAB + a_slots).astype(jnp.int32)
        picked = jnp.take(b_blocks, partner, axis=0)
        picked_cols = jnp.take(b_index, partner, axis=0)
        matches = (picked_cols[:, :, :, :, None] == c_index[:, None, :, None, :]).astype(jnp.float32)
        a_parts = a_vals.reshape(MB, BLK, KS, BLK)
        products = jnp.einsum("rmsj,rscjn->rcmsn", a_parts, picked, precision=lax.Precision.HIGHEST)
        products = products.reshape(MB, N_COL, BLK, KS, KB, BLK)
        placed = jnp.einsum("rcmsbq,rscbk->rcmkq", products, matches, precision=lax.Precision.HIGHEST)
        total = total + placed.reshape(MB, N_COL, BLK, KC * BLK)
        return total, None

    start = jnp.zeros((MB, N_COL, BLK, KC * BLK), jnp.float32)
    total, unused = lax.scan(visit, start, jnp.arange(NSLAB, dtype=jnp.int32))
    return total
```

```python
import functools

import jax
import jax.numpy as jnp
from jax import lax
from jax.experimental import pallas as pl
from jax.experimental.pallas import tpu as pltpu
from jax.sharding import PartitionSpec as P


def placed_kernel(dims, meta, a_idx, b_idx, m_idx, c_idx, a_end, a_mid, b_own, b_mate, send, keep,
                  a_buf, b_buf, p_buf, a_sem, b_sem):
    x, core, y, piece, take_mid = (meta[n] for n in range(5))
    halves, depths, steps, tiles, slabs, kept, per_row, window, slab = dims
    count = halves * depths * steps

    @pl.when(take_mid == 0)
    def _():
        pltpu.make_async_copy(a_end, a_buf, a_sem).start()

    @pl.when(take_mid != 0)
    def _():
        pltpu.make_async_copy(a_mid, a_buf, a_sem).start()

    my_tile = meta[5]
    rel_tile = jnp.bitwise_xor(my_tile, piece)

    def place(n):
        ex = 1 - n // (depths * steps)
        d = (n // steps) % depths
        t = n % steps
        e = jnp.bitwise_xor(y, d)
        local = piece * depths * steps + d * steps + t
        half = jnp.bitwise_xor(x, ex)
        return ex, e, t, local, half

    def slots_of(n):
        ex, e, t, local, half = place(n)
        base = ((rel_tile * depths + e) * halves + ex) * steps + t
        own_slab = (x * 2 + core) * depths + y
        mate_slab = (x * 2 + 1 - core) * depths + y
        at_own = (base * slabs + own_slab) * per_row
        at_mate = (base * slabs + mate_slab) * per_row
        row = half * 2 + core
        start = jnp.clip(row * (window - 2) - 1, 0, slab - window)
        own = [a_idx[at_own + s] for s in range(per_row)]
        mate = [a_idx[at_mate + s] - start for s in range(per_row)]
        return half, own, mate, start

    def fetch(n, _):
        half, own, mate, _s = slots_of(n)
        for s in range(per_row):
            pltpu.make_async_copy(b_own.at[own[s]], b_buf.at[n, s], b_sem.at[n, s]).start()
            pltpu.make_async_copy(
                b_mate.at[half, mate[s]], b_buf.at[n, per_row + s], b_sem.at[n, per_row + s]
            ).start()
        return 0

    lax.fori_loop(0, count, fetch, 0)
    pltpu.make_async_copy(a_end, a_buf, a_sem).wait()

    size = a_buf.shape[-2]
    wide = 2 * size
    low = lax.broadcasted_iota(jnp.int32, (8, wide), 1) < size

    def work(n, _):
        ex, e, t, local, half = place(n)
        _h, own, mate, start = slots_of(n)
        per_tile = tiles * depths * steps
        c_at = (jnp.where(ex == 0, 0, 1) * per_tile + local) * kept
        c_of = [jnp.where(low, c_idx[c_at + 2 * k], c_idx[c_at + 2 * k + 1]) for k in range(kept // 2)]
        for s in range(2 * per_row):
            pltpu.make_async_copy(b_own.at[0], b_buf.at[n, s], b_sem.at[n, s]).wait()
        for s in range(2 * per_row):
            if s < per_row:
                at = own[s] * 4
                cols = [b_idx[at + b] for b in range(4)]
            else:
                at = (mate[s - per_row] + start) * 4
                cols = [m_idx[at + b] for b in range(4)]
            from0 = jnp.where(low, cols[0], cols[1])
            turn0 = jnp.where(low, cols[1], cols[0])
            from1 = jnp.where(low, cols[2], cols[3])
            turn1 = jnp.where(low, cols[3], cols[2])
            for g in range(size // 8):
                v0 = b_buf[n, s, g * 8:(g + 1) * 8, :wide]
                v1 = b_buf[n, s, g * 8:(g + 1) * 8, wide:]
                r0 = pltpu.roll(v0, size, 1)
                r1 = pltpu.roll(v1, size, 1)
                for k in range(kept // 2):
                    got = (
                        jnp.where(from0 == c_of[k], v0, 0.0)
                        + jnp.where(turn0 == c_of[k], r0, 0.0)
                        + jnp.where(from1 == c_of[k], v1, 0.0)
                        + jnp.where(turn1 == c_of[k], r1, 0.0)
                    )
                    p_buf[s * size + g * 8:s * size + (g + 1) * 8, k * wide:(k + 1) * wide] = got
        a_row = jnp.concatenate(
            [a_buf[ex, e, t, core], a_buf[ex, e, t, 1 - core]], axis=1
        )
        a_hi = a_row.astype(jnp.bfloat16)
        a_lo = (a_row - a_hi.astype(jnp.float32)).astype(jnp.bfloat16)
        p_all = p_buf[...]
        p_hi = p_all.astype(jnp.bfloat16)
        p_lo = (p_all - p_hi.astype(jnp.float32)).astype(jnp.bfloat16)
        both = jnp.dot(jnp.concatenate([a_hi, a_lo], axis=0), p_hi, preferred_element_type=jnp.float32)
        out = both[:size] + (both[size:] + jnp.dot(a_hi, p_lo, preferred_element_type=jnp.float32))

        @pl.when(ex == 1)
        def _():
            send[n] = out

        @pl.when(ex == 0)
        def _():
            keep[n - depths * steps] = out

        return 0

    lax.fori_loop(0, count, work, 0)


def placed_products(dims, meta, a_idx, b_idx, m_idx, c_idx, a_end, a_mid, b_own, b_mate):
    halves, depths, steps, tiles, slabs, kept, per_row, window, slab = dims
    count = halves * depths * steps
    size = a_end.shape[-2]
    shape = jax.ShapeDtypeStruct((depths * steps, size, kept * size), jnp.float32)
    smem = pl.BlockSpec(memory_space=pltpu.SMEM)
    anywhere = pl.BlockSpec(memory_space=pl.ANY)
    vmem = pl.BlockSpec(memory_space=pltpu.VMEM)
    return pl.pallas_call(
        functools.partial(placed_kernel, dims),
        out_shape=(shape, shape),
        in_specs=[smem] * 5 + [anywhere] * 4,
        out_specs=(vmem, vmem),
        scratch_shapes=[
            pltpu.VMEM(a_end.shape, jnp.float32),
            pltpu.VMEM((count, 2 * per_row) + b_own.shape[1:], jnp.float32),
            pltpu.VMEM((2 * per_row * size, kept * size), jnp.float32),
            pltpu.SemaphoreType.DMA,
            pltpu.SemaphoreType.DMA((count, 2 * per_row)),
        ],
        compiler_params=pltpu.CompilerParams(vmem_limit_bytes=24 * 1024 * 1024),
        cost_estimate=pl.CostEstimate(
            flops=count * 6 * size * 2 * per_row * size * kept * size,
            bytes_accessed=count * (2 * per_row * 4 * size * size + kept * size * size + 2 * per_row * size * size) * 4,
            transcendentals=0,
        ),
    )(meta, a_idx, b_idx, m_idx, c_idx, a_end, a_mid, b_own, b_mate)


def on_device(a_blocks, a_index, b_blocks, b_index, c_index):
    rows = lax.axis_size("row")
    tiles = lax.axis_size("col")
    depths = lax.axis_size("depth")
    row = lax.axis_index("row")
    z = lax.axis_index("col")
    y = lax.axis_index("depth")
    x, core = row // 2, row % 2
    halves = rows // 2
    steps, slabs, size, a_width = a_blocks.shape
    per_row = a_index.shape[2]
    kept = c_index.shape[2]
    slab = b_blocks.shape[0]
    window = slab // rows + 2

    mates = [(r, r ^ 1) for r in range(rows)]
    across = [(r, r ^ 2) for r in range(rows)]

    b_own = b_blocks.reshape(slab, size, -1)
    starts = [jnp.clip((h * 2 + 1 - core) * (window - 2) - 1, 0, slab - window) for h in range(halves)]
    b_send = jnp.stack([lax.dynamic_slice_in_dim(b_own, s, window, 0) for s in starts])

    a_by = a_blocks.reshape(steps, halves, 2, depths, size, a_width)

    def a_for(ex, e):
        return lax.dynamic_index_in_dim(
            lax.dynamic_index_in_dim(a_by, x ^ ex, 1, keepdims=False), y ^ e, 2, keepdims=False
        )

    def doubled(value, axis, bit):
        return jnp.concatenate(
            [value, lax.ppermute(value, axis, [(i, i ^ bit) for i in range(lax.axis_size(axis))])]
        )

    first = jnp.concatenate([a_index.reshape(-1), c_index.reshape(-1)])
    pair = doubled(first[None], "row", 2)
    c_pair = pair[:, a_index.size:].reshape(-1)
    a_rel = pair[:, :a_index.size].reshape(-1)
    bit = 1
    while bit < depths:
        a_rel = doubled(a_rel, "depth", bit)
        bit *= 2
    bit = 1
    while bit < tiles:
        a_rel = doubled(a_rel, "col", bit)
        bit *= 2
    b_flat = b_index.reshape(-1)
    m_flat = lax.ppermute(b_flat, "row", mates)

    parts = []
    for ex in range(halves):
        for e in range(depths):
            part = a_for(ex, e)
            if ex or e:
                perm = [
                    (r * depths + d, (r ^ (2 * ex)) * depths + (d ^ e))
                    for r in range(rows)
                    for d in range(depths)
                ]
                part = lax.ppermute(part, ("row", "depth"), perm)
            parts.append(part)
    own = jnp.stack(parts).reshape(halves, depths, steps, 2, size, a_width)
    b_mate = lax.ppermute(b_send, "row", mates)

    near = lax.ppermute(own, "col", [(0, 1), (1, 0), (2, 3), (3, 2)])
    inner = lax.ppermute(own, "col", [(1, 2), (2, 1)])
    outer = lax.ppermute(inner, "col", [(1, 0), (2, 3)])
    through = lax.ppermute(near, "col", [(2, 1), (1, 2)])
    last = lax.ppermute(through, "col", [(1, 0), (2, 3)])

    middle = (z == 1) | (z == 2)
    sources = [(own, own), (near, near), (outer, inner), (last, through)]
    pieces = [z, z ^ 1, jnp.where(z < 2, 2, 1), jnp.where(z < 2, 3, 0)]
    table = [[0, 1, 2, 3], [1, 0, 3, 2], [2, 2, 1, 1], [3, 3, 0, 0]]
    dims = (halves, depths, steps, tiles, slabs, kept, per_row, window, slab)

    sums = []
    for slot in range(tiles):
        meta = jnp.stack([x, core, y, pieces[slot], middle.astype(jnp.int32), z]).astype(jnp.int32)
        send, keep = placed_products(
            dims, meta, a_rel, b_flat, m_flat, c_pair, *sources[slot], b_own, b_mate
        )
        half_sum = keep + lax.ppermute(send, "row", across)
        if depths == 2:
            perm = []
            for c in range(tiles):
                to = table[slot][c] * depths // tiles
                perm.append((c * depths + 1 - to, c * depths + to))
            sums.append(half_sum + lax.ppermute(half_sum, ("col", "depth"), perm))
        else:
            sums.append(lax.psum(half_sum, "depth"))

    if depths == 2:
        mine = (y * tiles // depths) == (z // 2 * 2)
        one = jnp.where(mine, sums[0], sums[2])
        two = jnp.where(mine, sums[1], sums[3])
        one_piece = jnp.where(mine, pieces[0], pieces[2])
        swap = one_piece % 2 == 1
        out = jnp.concatenate([jnp.where(swap, two, one), jnp.where(swap, one, two)])
    else:
        full = jnp.zeros((tiles,) + sums[0].shape, jnp.float32)
        for slot in range(tiles):
            full = lax.dynamic_update_index_in_dim(full, sums[slot], pieces[slot], 0)
        full = full.reshape((-1,) + sums[0].shape[1:])
        share = full.shape[0] // depths
        out = lax.dynamic_slice_in_dim(full, y * share, share, 0)
    return out[:, None]


def solution(mesh):
    return jax.shard_map(
        on_device,
        mesh=mesh,
        in_specs=(
            P(("row", "col", "depth"), None, None, None),
            P(("row", "col", "depth"), None, None),
            P(("row", "depth"), "col", None, None),
            P(("row", "depth"), "col", None),
            P("row", "col", None),
        ),
        out_specs=P(("row", "depth"), "col", None, None),
        check_vma=False,
    )
```

```python
import functools

import jax
import jax.numpy as jnp
from jax import lax
from jax.experimental import pallas as pl
from jax.experimental.pallas import tpu as pltpu
from jax.sharding import PartitionSpec as P

LANES = 128
INDEX_ROWS = 8
COST = 1000000000
VMEM_BYTES = 48 * 1024 * 1024
CUTS = (1, 1, 2, 2)
Y_WITH = {0: 1, 1: 3, 2: 4, 3: 5, 4: 5, 5: 5}
SETTLE = {6: [0, 1, 2, 3, 4, 5]}


def slot_piece(slot, z, tiles):
    if slot == 0:
        return z
    if slot == 1:
        return jnp.bitwise_xor(z, 1)
    if slot == 2:
        return jnp.where(z < tiles // 2, 2, 1)
    return jnp.where(z < tiles // 2, 3, 0)


def placed_kernel(dims, slot, first, count, across, table, a_refs, b_own, b_mate, after, send, keep,
                  a_buf, i_wide, i_whole, i_buf, b_buf, p_hi, p_lo, a_sem, i_sem, b_sem):
    halves, depths, steps, tiles, kept, per_row, b_count, slab, size, near_rows = dims
    x, core, y, z = (table[n] for n in range(4))
    at_mine, at_mate = 8, 8 + slab * b_count
    at_kept = at_mate + slab * b_count
    data_rows = steps * 2 * size
    part_rows = data_rows + INDEX_ROWS
    wide = 2 * size
    per_piece = depths * steps
    per_tile = tiles * per_piece
    piece = slot_piece(slot, z, tiles)
    middle = jnp.logical_and(z > 0, z < tiles - 1)

    def loads(refs):
        index, copies = [], []
        which = 0
        for ref in refs:
            for part in range(ref.shape[0] // part_rows):
                index.append(
                    pltpu.make_async_copy(
                        ref.at[pl.ds(part * part_rows + data_rows, INDEX_ROWS)],
                        i_wide.at[pl.ds(which * INDEX_ROWS, INDEX_ROWS)],
                        i_sem.at[which],
                    )
                )
                copies.append(
                    pltpu.make_async_copy(
                        ref.at[pl.ds(part * part_rows, data_rows)],
                        a_buf.at[pl.ds(which * data_rows, data_rows)],
                        a_sem.at[which],
                    )
                )
                which += 1
        return index + copies

    starts, rows = [], []
    for ex in range(halves):
        block_row = (jnp.bitwise_xor(x, ex) * 2 + core) * per_tile + piece * per_piece + first
        start = jnp.clip(block_row * slab // (halves * 2 * per_tile) - 1, 0, slab - near_rows)
        band = pl.ds(pl.multiple_of(start * size, size), near_rows * size)
        rows.append(
            [
                pltpu.make_async_copy(source.at[band], b_buf.at[ex, number], b_sem.at[ex, number])
                for number, source in enumerate((b_own, b_mate))
            ]
        )
        starts.append(start)
    for ex in reversed(range(halves)):
        for copy in rows[ex]:
            copy.start()
    if len(a_refs) == 1:
        data = loads(a_refs[0])
        for copy in data:
            copy.start()
    else:
        @pl.when(middle)
        def _():
            for copy in loads(a_refs[1]):
                copy.start()

        @pl.when(jnp.logical_not(middle))
        def _():
            for copy in loads(a_refs[0]):
                copy.start()

        data = loads(a_refs[0])
    for copy in data[:halves * across]:
        copy.wait()
    data = data[halves * across:]
    i_whole[...] = i_wide[...].astype(jnp.int32)
    whole = pltpu.make_async_copy(i_whole, i_buf, i_sem.at[halves * across])
    whole.start()
    whole.wait()

    low = lax.broadcasted_iota(jnp.int32, (8, wide), 1) < size

    def place(n):
        d = (first + n) // steps
        return jnp.bitwise_xor(y, d) % across, (first + n) % steps

    def build(ex, n, high, low_part):
        e, t = place(n)
        c_at = at_kept + (ex * per_tile + piece * per_piece + first + n) * kept
        c_of = [jnp.where(low, table[c_at + 2 * k], table[c_at + 2 * k + 1]) for k in range(kept // 2)]
        for s in range(2 * per_row):
            whose = core if s < per_row else 1 - core
            row = i_buf[(ex * across + e) * INDEX_ROWS, (t * 2 + whose) * per_row + s % per_row]
            at = (at_mine if s < per_row else at_mate) + row * b_count
            cols = [table[at + b] for b in range(b_count)]
            held_at = pl.multiple_of((row - starts[ex]) * size, size)
            wanted = []
            for b in range(0, b_count, 2):
                wanted.append(jnp.where(low, cols[b], cols[b + 1]))
                wanted.append(jnp.where(low, cols[b + 1], cols[b]))
            held = []
            for g in range(size // 8):
                row = []
                for b in range(b_count // 2):
                    v = b_buf[ex, s // per_row, pl.ds(held_at + g * 8, 8), b * wide:(b + 1) * wide]
                    row += [v, pltpu.roll(v, size, 1)]
                held.append(row)
            for k in range(kept // 2):
                masks = [w == c_of[k] for w in wanted]
                for pair in range(size // 16):
                    both = []
                    for g in (2 * pair, 2 * pair + 1):
                        got = jnp.where(masks[0], held[g][0], 0.0)
                        for m in range(1, b_count):
                            got = got + jnp.where(masks[m], held[g][m], 0.0)
                        both.append(got)
                    both = jnp.concatenate(both, axis=0)
                    hi = both.astype(jnp.bfloat16)
                    lo = (both - hi.astype(jnp.float32)).astype(jnp.bfloat16)
                    rows = slice(s * size + pair * 16, s * size + (pair + 1) * 16)
                    high[rows, k * wide:(k + 1) * wide] = hi
                    low_part[rows, k * wide:(k + 1) * wide] = lo

    def multiply(ex, n, high, low_part):
        e, t = place(n)
        base = (ex * across + e) * data_rows + t * 2 * size
        a_row = jnp.concatenate(
            [
                a_buf[pl.ds(pl.multiple_of(base + core * size, size), size)],
                a_buf[pl.ds(pl.multiple_of(base + (1 - core) * size, size), size)],
            ],
            axis=1,
        )
        a_hi = a_row.astype(jnp.bfloat16)
        a_lo = (a_row - a_hi.astype(jnp.float32)).astype(jnp.bfloat16)
        both = jnp.dot(jnp.concatenate([a_hi, a_lo], axis=0), high[...], preferred_element_type=jnp.float32)
        return both[:size] + (both[size:] + jnp.dot(a_hi, low_part[...], preferred_element_type=jnp.float32))

    for ex in reversed(range(halves)):
        for copy in rows[ex]:
            copy.wait()
        if ex == halves - 1:
            for copy in data:
                copy.wait()

        def two(m, _, ex=ex):
            for u in range(2):
                build(ex, 2 * m + u, p_hi[u], p_lo[u])
            for u in range(2):
                out = multiply(ex, 2 * m + u, p_hi[u], p_lo[u])
                if ex:
                    send[2 * m + u] = out
                else:
                    keep[2 * m + u] = out
            return 0

        lax.fori_loop(0, count // 2, two, 0)


def placed_products(dims, slot, first, count, across, table, a_sources, b_own, b_mate, after):
    halves, depths, steps, tiles, kept, per_row, b_count, slab, size, near_rows = dims
    shape = jax.ShapeDtypeStruct((count, size, kept * size), jnp.float32)
    smem = pl.BlockSpec(memory_space=pltpu.SMEM)
    anywhere = pl.BlockSpec(memory_space=pl.ANY)
    hbm = pl.BlockSpec(memory_space=pltpu.HBM)
    vmem = pl.BlockSpec(memory_space=pltpu.VMEM)
    parts = halves * across
    placed_shape = pltpu.VMEM((2 * per_row * size, kept * size), jnp.bfloat16)
    return pl.pallas_call(
        functools.partial(placed_kernel, dims, slot, first, count, across),
        out_shape=(shape, shape),
        in_specs=[smem] + [jax.tree.map(lambda _: anywhere, a_sources), hbm, hbm, [anywhere] * len(after)],
        out_specs=(vmem, vmem),
        scratch_shapes=[
            pltpu.VMEM((parts * steps * 2 * size, LANES), jnp.float32),
            pltpu.VMEM((parts * INDEX_ROWS, LANES), jnp.float32),
            pltpu.VMEM((parts * INDEX_ROWS, LANES), jnp.int32),
            pltpu.SMEM((parts * INDEX_ROWS, LANES), jnp.int32),
            pltpu.VMEM((halves, 2, near_rows * size, b_own.shape[1]), jnp.float32),
            [placed_shape] * 2,
            [placed_shape] * 2,
            pltpu.SemaphoreType.DMA((parts,)),
            pltpu.SemaphoreType.DMA((parts + 1,)),
            pltpu.SemaphoreType.DMA((halves, 2)),
        ],
        compiler_params=pltpu.CompilerParams(vmem_limit_bytes=VMEM_BYTES),
        cost_estimate=pl.CostEstimate(
            flops=COST * count * halves,
            bytes_accessed=4 * (2 * count * size * kept * size + parts * steps * 2 * size * LANES),
            transcendentals=0,
        ),
    )(table, a_sources, b_own, b_mate, after)


def joined_kernel(parts, after, out, sem):
    copies = []
    at = 0
    for number, part in enumerate(parts):
        copies.append(pltpu.make_async_copy(part, out.at[pl.ds(at, part.shape[0])], sem.at[number]))
        at += part.shape[0]
    for copy in copies:
        copy.start()
    for copy in copies:
        copy.wait()


def joined(parts, after):
    anywhere = pl.BlockSpec(memory_space=pl.ANY)
    total = sum(part.shape[0] for part in parts)
    return pl.pallas_call(
        joined_kernel,
        out_shape=jax.ShapeDtypeStruct((total,) + parts[0].shape[1:], jnp.float32),
        in_specs=[[anywhere] * len(parts), [anywhere] * len(after)],
        out_specs=pl.BlockSpec(memory_space=pltpu.VMEM),
        scratch_shapes=[pltpu.SemaphoreType.DMA((len(parts),))],
        compiler_params=pltpu.CompilerParams(vmem_limit_bytes=VMEM_BYTES),
        cost_estimate=pl.CostEstimate(flops=0, bytes_accessed=8 * total * LANES, transcendentals=0),
    )(parts, after)


def settle_kernel(slot, first, depths, steps, tiles, table, total, other, *refs):
    out, held, sem = refs[-3:]
    y, z = table[2], table[3]
    piece = slot_piece(slot, z, tiles)

    @pl.when(piece * depths // tiles == y)
    def _():
        held[...] = total[...] + other[...]
        at = piece % (tiles // depths) * depths * steps + first
        copy = pltpu.make_async_copy(held, out.at[pl.ds(at, total.shape[0]), 0], sem)
        copy.start()
        copy.wait()


def settled(slot, first, depths, steps, tiles, meta, total, other, out):
    anywhere = pl.BlockSpec(memory_space=pl.ANY)
    vmem = pl.BlockSpec(memory_space=pltpu.VMEM)
    shape = jax.ShapeDtypeStruct((tiles * steps, 1) + total.shape[1:], jnp.float32)
    so_far = [] if out is None else [out]
    return pl.pallas_call(
        functools.partial(settle_kernel, slot, first, depths, steps, tiles),
        out_shape=shape,
        in_specs=[pl.BlockSpec(memory_space=pltpu.SMEM), vmem, vmem] + [anywhere] * len(so_far),
        out_specs=anywhere,
        scratch_shapes=[pltpu.VMEM(total.shape, jnp.float32), pltpu.SemaphoreType.DMA],
        input_output_aliases={3: 0} if so_far else {},
        compiler_params=pltpu.CompilerParams(vmem_limit_bytes=VMEM_BYTES),
        cost_estimate=pl.CostEstimate(flops=0, bytes_accessed=12 * total.size, transcendentals=0),
    )(meta, total, other, *so_far)


def gate_kernel(value, after, out):
    pass


def gated(value, after):
    anywhere = pl.BlockSpec(memory_space=pl.ANY)
    return pl.pallas_call(
        gate_kernel,
        out_shape=jax.ShapeDtypeStruct(value.shape, value.dtype),
        in_specs=[anywhere, [anywhere] * len(after)],
        out_specs=anywhere,
        input_output_aliases={0: 0},
        cost_estimate=pl.CostEstimate(flops=0, bytes_accessed=0, transcendentals=0),
    )(value, after)


def sum_kernel(one, two, after, out):
    out[...] = one[...] + two[...]


def summed(one, two, after):
    vmem = pl.BlockSpec(memory_space=pltpu.VMEM)
    return pl.pallas_call(
        sum_kernel,
        out_shape=jax.ShapeDtypeStruct(one.shape, one.dtype),
        in_specs=[vmem, vmem, [pl.BlockSpec(memory_space=pl.ANY)] * len(after)],
        out_specs=vmem,
        compiler_params=pltpu.CompilerParams(vmem_limit_bytes=VMEM_BYTES),
        cost_estimate=pl.CostEstimate(flops=one.size, bytes_accessed=12 * one.size, transcendentals=0),
    )(one, two, after)


def split_kernel(halves, depths, cuts, meta, value, after, *refs):
    outs, sem = refs[:cuts], refs[cuts]
    y = meta[2]
    across = depths // cuts
    length = value.shape[0] // (halves * cuts)
    copies = []
    for ex in range(halves):
        for cut in range(cuts):
            at = pl.multiple_of((ex * cuts + jnp.bitwise_xor(y // across, cut)) * length, 8)
            copies.append(
                pltpu.make_async_copy(
                    value.at[pl.ds(at, length)], outs[cut].at[pl.ds(ex * length, length)], sem.at[ex, cut]
                )
            )
    for copy in copies:
        copy.start()
    for copy in copies:
        copy.wait()


def split(halves, depths, cuts, meta, value, after):
    anywhere = pl.BlockSpec(memory_space=pl.ANY)
    shape = jax.ShapeDtypeStruct((value.shape[0] // cuts, value.shape[1]), value.dtype)
    return pl.pallas_call(
        functools.partial(split_kernel, halves, depths, cuts),
        out_shape=(shape,) * cuts,
        in_specs=[pl.BlockSpec(memory_space=pltpu.SMEM), anywhere, [anywhere] * len(after)],
        out_specs=(pl.BlockSpec(memory_space=pltpu.VMEM),) * cuts,
        scratch_shapes=[pltpu.SemaphoreType.DMA((halves, cuts))],
        compiler_params=pltpu.CompilerParams(vmem_limit_bytes=VMEM_BYTES),
        cost_estimate=pl.CostEstimate(flops=0, bytes_accessed=8 * value.size, transcendentals=0),
    )(meta, value, after)


def along(value, step):
    pairs = {
        "near": [(0, 1), (1, 0), (2, 3), (3, 2)],
        "inner": [(1, 2), (2, 1)],
        "outer": [(1, 0), (2, 3)],
        "through": [(2, 1), (1, 2)],
        "last": [(1, 0), (2, 3)],
    }
    with jax.named_scope(step):
        return lax.ppermute(value, "col", pairs[step])


def on_device(a_blocks, a_index, b_blocks, b_index, c_index):
    rows = lax.axis_size("row")
    tiles = lax.axis_size("col")
    depths = lax.axis_size("depth")
    row = lax.axis_index("row")
    z = lax.axis_index("col")
    y = lax.axis_index("depth")
    x, core = row // 2, row % 2
    halves = rows // 2
    steps, slabs, size, a_width = a_blocks.shape
    per_row = a_index.shape[2]
    b_count = b_index.shape[2]
    kept = c_index.shape[2]
    slab = b_blocks.shape[0]
    meta = jnp.stack([x, core, y, z]).astype(jnp.int32)

    mates = [(r, r ^ 1) for r in range(rows)]
    across = [(r, r ^ 2) for r in range(rows)]

    b_own = b_blocks.reshape(slab * size, -1)
    b_flat = b_index.reshape(-1)
    with jax.named_scope("mate"):
        b_mate = lax.ppermute(b_own, "row", mates)
    with jax.named_scope("mate_index"):
        m_flat = lax.ppermute(b_flat, "row", mates)

    a_by = a_blocks.reshape(steps, halves, 2, depths, size, a_width)
    i_by = a_index.reshape(steps, halves, 2, depths, per_row).astype(jnp.float32)
    c_rows = c_index.reshape(-1).astype(jnp.float32)
    c_rows = jnp.pad(c_rows, (0, (INDEX_ROWS - 1) * LANES - c_rows.size)).reshape(-1, LANES)

    def a_for(ex, e):
        def pick(value):
            value = lax.dynamic_index_in_dim(value, x ^ ex, 1, keepdims=False)
            return lax.dynamic_index_in_dim(value, y ^ e, 2, keepdims=False)

        index = pick(i_by).reshape(1, -1)
        index = jnp.pad(index, ((0, 0), (0, LANES - index.shape[1])))
        return jnp.concatenate([pick(a_by).reshape(-1, LANES), index, c_rows])

    own = a_for(0, 0)
    others = [own]
    for ex in range(halves):
        for e in range(depths):
            if ex or e:
                perm = [
                    (r * depths + d, (r ^ (2 * ex)) * depths + (d ^ e))
                    for r in range(rows)
                    for d in range(depths)
                ]
                with jax.named_scope(f"spread_{ex}{e}"):
                    others.append(lax.ppermute(a_for(ex, e), ("row", "depth"), perm))
    c_across = others[depths][1 - INDEX_ROWS:].reshape(-1)[:c_index.size].astype(jnp.int32)
    with jax.named_scope("joined"):
        here = joined(others, [])
    near, inner = along(here, "near"), along(here, "inner")
    whole_table = jnp.concatenate(
        [jnp.pad(meta, (0, 4)), b_flat, m_flat, c_index.reshape(-1), c_across]
    )

    table = [[0, 1, 2, 3], [1, 0, 3, 2], [2, 2, 1, 1], [3, 3, 0, 0]]
    per_piece = depths * steps
    part_rows = own.shape[0]
    data_rows = part_rows - INDEX_ROWS
    block_rows = rows * tiles * per_piece

    x_sums, settle, pending, order = [], [], [], []
    out = None
    number = 0
    for slot in range(tiles):
        if slot == 0:
            a_sources = [[[here]]]
        elif slot == 1:
            near = gated(near, order)
            outer, through = along(inner, "outer"), along(near, "through")
            a_sources = [[[near]]]
        elif slot == 2:
            a_sources = [[[outer], [inner]]]
            throughs = split(halves, depths, CUTS[3], meta, through, order + [outer])
            lasts = [along(value, "last") for value in throughs]
        else:
            a_sources = [[[there], [here]] for there, here in zip(lasts, throughs)]
        cuts = CUTS[slot]
        count = per_piece // cuts
        near_rows = -(-count * slab // block_rows) + 2
        dims = (halves, depths, steps, tiles, kept, per_row, b_count, slab, size, near_rows)
        for cut in range(cuts):
            after = list(order)
            if depths == 2:
                for n in SETTLE.get(number, []):
                    out = settled(*settle[n], out)
                    after.append(out)
            across_here = depths if len(a_sources) == 1 else depths // cuts
            with jax.named_scope(f"placed_{slot}{cut}"):
                send, keep = placed_products(
                    dims, slot, cut * count, count, across_here, whole_table, a_sources[cut % len(a_sources)], b_own, b_mate, after
                )
            order = [keep]
            with jax.named_scope(f"x_{slot}{cut}"):
                other = lax.ppermute(send, "row", across)
            x_sums.append((keep, other))
            if depths == 2:
                perm = []
                for c in range(tiles):
                    to = table[slot][c] * depths // tiles
                    perm.append((c * depths + 1 - to, c * depths + to))
                settle.append(None)
                pending.append((number, slot, cut, count, perm))
                for item in [p for p in pending if Y_WITH[p[0]] <= number]:
                    pending.remove(item)
                    n, its_slot, its_cut, its_count, its_perm = item
                    with jax.named_scope(f"sum_{its_slot}{its_cut}"):
                        total = summed(*x_sums[n], order)
                    with jax.named_scope(f"y_{its_slot}{its_cut}"):
                        other = lax.ppermute(total, ("col", "depth"), its_perm)
                    settle[n] = (its_slot, its_cut * its_count, depths, steps, tiles, meta, total, other)
            number += 1

    if depths == 2:
        for n in SETTLE[number]:
            out = settled(*settle[n], out)
    if depths != 2:
        full = jnp.zeros((tiles, per_piece) + x_sums[0][0].shape[1:], jnp.float32)
        at = 0
        for slot in range(tiles):
            total = lax.psum(jnp.concatenate([one + two for one, two in x_sums[at:at + CUTS[slot]]]), "depth")
            at += CUTS[slot]
            full = lax.dynamic_update_index_in_dim(full, total, slot_piece(slot, z, tiles), 0)
        full = full.reshape((tiles * per_piece,) + x_sums[0][0].shape[1:])
        share = full.shape[0] // depths
        out = lax.dynamic_slice_in_dim(full, y * share, share, 0)[:, None]
    return out


def solution(mesh):
    return jax.shard_map(
        on_device,
        mesh=mesh,
        in_specs=(
            P(("row", "col", "depth"), None, None, None),
            P(("row", "col", "depth"), None, None),
            P(("row", "depth"), "col", None, None),
            P(("row", "depth"), "col", None),
            P("row", "col", None),
        ),
        out_specs=P(("row", "depth"), "col", None, None),
        check_vma=False,
    )
```

```python
import functools

import jax
import jax.numpy as jnp
from jax import lax
from jax.experimental import pallas as pl
from jax.experimental.pallas import tpu as pltpu
from jax.sharding import PartitionSpec as P

LANES = 128
INDEX_ROWS = 8
COST = 1000000000
VMEM_BYTES = 48 * 1024 * 1024
CUTS = (1, 1, 2, 2)
Y_WITH = {0: 1, 1: 2, 2: 3, 3: 4, 4: 5, 5: 5}
BEFORE_SUM = {5: [2]}
BEFORE_OTHER = {4: [0]}
SUM_AFTER = {4: [1, 2], 5: [3]}


def slot_piece(slot, z, tiles):
    if slot == 0:
        return z
    if slot == 1:
        return jnp.bitwise_xor(z, 1)
    if slot == 2:
        return jnp.where(z < tiles // 2, 2, 1)
    return jnp.where(z < tiles // 2, 3, 0)


def placed_kernel(dims, slot, first, count, across, table, a_refs, b_own, b_mate, after, send, keep,
                  a_buf, i_wide, i_whole, i_buf, b_buf, p_hi, p_lo, a_sem, i_sem, b_sem):
    halves, depths, steps, tiles, kept, per_row, b_count, slab, size, near_rows = dims
    x, core, y, z = (table[n] for n in range(4))
    at_mine, at_mate = 8, 8 + slab * b_count
    at_kept = at_mate + slab * b_count
    data_rows = steps * 2 * size
    part_rows = data_rows + INDEX_ROWS
    wide = 2 * size
    per_piece = depths * steps
    per_tile = tiles * per_piece
    piece = slot_piece(slot, z, tiles)
    middle = jnp.logical_and(z > 0, z < tiles - 1)

    def loads(refs):
        index, copies = [], []
        which = 0
        for ref in refs:
            for part in range(ref.shape[0] // part_rows):
                index.append(
                    pltpu.make_async_copy(
                        ref.at[pl.ds(part * part_rows + data_rows, INDEX_ROWS)],
                        i_wide.at[pl.ds(which * INDEX_ROWS, INDEX_ROWS)],
                        i_sem.at[which],
                    )
                )
                copies.append(
                    pltpu.make_async_copy(
                        ref.at[pl.ds(part * part_rows, data_rows)],
                        a_buf.at[pl.ds(which * data_rows, data_rows)],
                        a_sem.at[which],
                    )
                )
                which += 1
        return index + copies

    starts, rows = [], []
    for ex in range(halves):
        block_row = (jnp.bitwise_xor(x, ex) * 2 + core) * per_tile + piece * per_piece + first
        start = jnp.clip(block_row * slab // (halves * 2 * per_tile) - 1, 0, slab - near_rows)
        band = pl.ds(pl.multiple_of(start * size, size), near_rows * size)
        rows.append(
            [
                pltpu.make_async_copy(source.at[band], b_buf.at[ex, number], b_sem.at[ex, number])
                for number, source in enumerate((b_own, b_mate))
            ]
        )
        starts.append(start)
    for ex in reversed(range(halves)):
        for copy in rows[ex]:
            copy.start()
    if len(a_refs) == 1:
        data = loads(a_refs[0])
        for copy in data:
            copy.start()
    else:
        @pl.when(middle)
        def _():
            for copy in loads(a_refs[1]):
                copy.start()

        @pl.when(jnp.logical_not(middle))
        def _():
            for copy in loads(a_refs[0]):
                copy.start()

        data = loads(a_refs[0])
    for copy in data[:halves * across]:
        copy.wait()
    data = data[halves * across:]
    i_whole[...] = i_wide[...].astype(jnp.int32)
    whole = pltpu.make_async_copy(i_whole, i_buf, i_sem.at[halves * across])
    whole.start()
    whole.wait()

    low = lax.broadcasted_iota(jnp.int32, (8, wide), 1) < size

    def place(n):
        d = (first + n) // steps
        return jnp.bitwise_xor(y, d) % across, (first + n) % steps

    def build(ex, n, high, low_part):
        e, t = place(n)
        c_at = at_kept + (ex * per_tile + piece * per_piece + first + n) * kept
        c_of = [jnp.where(low, table[c_at + 2 * k], table[c_at + 2 * k + 1]) for k in range(kept // 2)]
        for s in range(2 * per_row):
            whose = core if s < per_row else 1 - core
            row = i_buf[(ex * across + e) * INDEX_ROWS, (t * 2 + whose) * per_row + s % per_row]
            at = (at_mine if s < per_row else at_mate) + row * b_count
            cols = [table[at + b] for b in range(b_count)]
            held_at = pl.multiple_of((row - starts[ex]) * size, size)
            wanted = []
            for b in range(0, b_count, 2):
                wanted.append(jnp.where(low, cols[b], cols[b + 1]))
                wanted.append(jnp.where(low, cols[b + 1], cols[b]))
            held = []
            for g in range(size // 8):
                row = []
                for b in range(b_count // 2):
                    v = b_buf[ex, s // per_row, pl.ds(held_at + g * 8, 8), b * wide:(b + 1) * wide]
                    row += [v, pltpu.roll(v, size, 1)]
                held.append(row)
            for k in range(kept // 2):
                masks = [w == c_of[k] for w in wanted]
                for pair in range(size // 16):
                    both = []
                    for g in (2 * pair, 2 * pair + 1):
                        got = jnp.where(masks[0], held[g][0], 0.0)
                        for m in range(1, b_count):
                            got = got + jnp.where(masks[m], held[g][m], 0.0)
                        both.append(got)
                    both = jnp.concatenate(both, axis=0)
                    hi = both.astype(jnp.bfloat16)
                    lo = (both - hi.astype(jnp.float32)).astype(jnp.bfloat16)
                    rows = slice(s * size + pair * 16, s * size + (pair + 1) * 16)
                    high[rows, k * wide:(k + 1) * wide] = hi
                    low_part[rows, k * wide:(k + 1) * wide] = lo

    def multiply(ex, n, high, low_part):
        e, t = place(n)
        base = (ex * across + e) * data_rows + t * 2 * size
        a_row = jnp.concatenate(
            [
                a_buf[pl.ds(pl.multiple_of(base + core * size, size), size)],
                a_buf[pl.ds(pl.multiple_of(base + (1 - core) * size, size), size)],
            ],
            axis=1,
        )
        a_hi = a_row.astype(jnp.bfloat16)
        a_lo = (a_row - a_hi.astype(jnp.float32)).astype(jnp.bfloat16)
        both = jnp.dot(jnp.concatenate([a_hi, a_lo], axis=0), high[...], preferred_element_type=jnp.float32)
        return both[:size] + (both[size:] + jnp.dot(a_hi, low_part[...], preferred_element_type=jnp.float32))

    for ex in reversed(range(halves)):
        for copy in rows[ex]:
            copy.wait()
        if ex == halves - 1:
            for copy in data:
                copy.wait()

        def two(m, _, ex=ex):
            for u in range(2):
                build(ex, 2 * m + u, p_hi[u], p_lo[u])
            for u in range(2):
                out = multiply(ex, 2 * m + u, p_hi[u], p_lo[u])
                if ex:
                    send[2 * m + u] = out
                else:
                    keep[2 * m + u] = out
            return 0

        lax.fori_loop(0, count // 2, two, 0)


def placed_products(dims, slot, first, count, across, table, a_sources, b_own, b_mate, after):
    halves, depths, steps, tiles, kept, per_row, b_count, slab, size, near_rows = dims
    shape = jax.ShapeDtypeStruct((count, size, kept * size), jnp.float32)
    smem = pl.BlockSpec(memory_space=pltpu.SMEM)
    anywhere = pl.BlockSpec(memory_space=pl.ANY)
    hbm = pl.BlockSpec(memory_space=pltpu.HBM)
    vmem = pl.BlockSpec(memory_space=pltpu.VMEM)
    parts = halves * across
    placed_shape = pltpu.VMEM((2 * per_row * size, kept * size), jnp.bfloat16)
    return pl.pallas_call(
        functools.partial(placed_kernel, dims, slot, first, count, across),
        out_shape=(shape, shape),
        in_specs=[smem] + [jax.tree.map(lambda _: anywhere, a_sources), hbm, hbm, [anywhere] * len(after)],
        out_specs=(vmem, vmem),
        scratch_shapes=[
            pltpu.VMEM((parts * steps * 2 * size, LANES), jnp.float32),
            pltpu.VMEM((parts * INDEX_ROWS, LANES), jnp.float32),
            pltpu.VMEM((parts * INDEX_ROWS, LANES), jnp.int32),
            pltpu.SMEM((parts * INDEX_ROWS, LANES), jnp.int32),
            pltpu.VMEM((halves, 2, near_rows * size, b_own.shape[1]), jnp.float32),
            [placed_shape] * 2,
            [placed_shape] * 2,
            pltpu.SemaphoreType.DMA((parts,)),
            pltpu.SemaphoreType.DMA((parts + 1,)),
            pltpu.SemaphoreType.DMA((halves, 2)),
        ],
        compiler_params=pltpu.CompilerParams(vmem_limit_bytes=VMEM_BYTES),
        cost_estimate=pl.CostEstimate(
            flops=COST * count * halves,
            bytes_accessed=4 * (2 * count * size * kept * size + parts * steps * 2 * size * LANES),
            transcendentals=0,
        ),
    )(table, a_sources, b_own, b_mate, after)


def joined_kernel(parts, after, out, sem):
    copies = []
    at = 0
    for number, part in enumerate(parts):
        copies.append(pltpu.make_async_copy(part, out.at[pl.ds(at, part.shape[0])], sem.at[number]))
        at += part.shape[0]
    for copy in copies:
        copy.start()
    for copy in copies:
        copy.wait()


def joined(parts, after):
    anywhere = pl.BlockSpec(memory_space=pl.ANY)
    total = sum(part.shape[0] for part in parts)
    return pl.pallas_call(
        joined_kernel,
        out_shape=jax.ShapeDtypeStruct((total,) + parts[0].shape[1:], jnp.float32),
        in_specs=[[anywhere] * len(parts), [anywhere] * len(after)],
        out_specs=pl.BlockSpec(memory_space=pltpu.VMEM),
        scratch_shapes=[pltpu.SemaphoreType.DMA((len(parts),))],
        compiler_params=pltpu.CompilerParams(vmem_limit_bytes=VMEM_BYTES),
        cost_estimate=pl.CostEstimate(flops=0, bytes_accessed=8 * total * LANES, transcendentals=0),
    )(parts, after)


def settle_kernel(slot, first, depths, steps, tiles, table, total, other, *refs):
    out, held, sem = refs[-3:]
    y, z = table[2], table[3]
    piece = slot_piece(slot, z, tiles)

    @pl.when(piece * depths // tiles == y)
    def _():
        held[...] = total[...] + other[...]
        at = piece % (tiles // depths) * depths * steps + first
        copy = pltpu.make_async_copy(held, out.at[pl.ds(at, total.shape[0]), 0], sem)
        copy.start()
        copy.wait()


def settled(slot, first, depths, steps, tiles, meta, total, other, out):
    anywhere = pl.BlockSpec(memory_space=pl.ANY)
    vmem = pl.BlockSpec(memory_space=pltpu.VMEM)
    shape = jax.ShapeDtypeStruct((tiles * steps, 1) + total.shape[1:], jnp.float32)
    so_far = [] if out is None else [out]
    return pl.pallas_call(
        functools.partial(settle_kernel, slot, first, depths, steps, tiles),
        out_shape=shape,
        in_specs=[pl.BlockSpec(memory_space=pltpu.SMEM), vmem, vmem] + [anywhere] * len(so_far),
        out_specs=anywhere,
        scratch_shapes=[pltpu.VMEM(total.shape, jnp.float32), pltpu.SemaphoreType.DMA],
        input_output_aliases={3: 0} if so_far else {},
        compiler_params=pltpu.CompilerParams(vmem_limit_bytes=VMEM_BYTES),
        cost_estimate=pl.CostEstimate(flops=0, bytes_accessed=12 * total.size, transcendentals=0),
    )(meta, total, other, *so_far)


def gate_kernel(value, after, out):
    pass


def gated(value, after):
    anywhere = pl.BlockSpec(memory_space=pl.ANY)
    return pl.pallas_call(
        gate_kernel,
        out_shape=jax.ShapeDtypeStruct(value.shape, value.dtype),
        in_specs=[anywhere, [anywhere] * len(after)],
        out_specs=anywhere,
        input_output_aliases={0: 0},
        cost_estimate=pl.CostEstimate(flops=0, bytes_accessed=0, transcendentals=0),
    )(value, after)


def sum_kernel(one, two, after, out):
    out[...] = one[...] + two[...]


def summed(one, two, after):
    vmem = pl.BlockSpec(memory_space=pltpu.VMEM)
    return pl.pallas_call(
        sum_kernel,
        out_shape=jax.ShapeDtypeStruct(one.shape, one.dtype),
        in_specs=[vmem, vmem, [pl.BlockSpec(memory_space=pl.ANY)] * len(after)],
        out_specs=vmem,
        compiler_params=pltpu.CompilerParams(vmem_limit_bytes=VMEM_BYTES),
        cost_estimate=pl.CostEstimate(flops=one.size, bytes_accessed=12 * one.size, transcendentals=0),
    )(one, two, after)


def taken_kernel(halves, depths, cuts, cut, meta, value, after, out, sem):
    y = meta[2]
    length = value.shape[0] // (halves * cuts)
    copies = []
    for ex in range(halves):
        at = pl.multiple_of((ex * cuts + jnp.bitwise_xor(y // (depths // cuts), cut)) * length, 8)
        copies.append(pltpu.make_async_copy(value.at[pl.ds(at, length)], out.at[pl.ds(ex * length, length)], sem.at[ex]))
    for copy in copies:
        copy.start()
    for copy in copies:
        copy.wait()


def taken(halves, depths, cuts, cut, meta, value, after):
    anywhere = pl.BlockSpec(memory_space=pl.ANY)
    return pl.pallas_call(
        functools.partial(taken_kernel, halves, depths, cuts, cut),
        out_shape=jax.ShapeDtypeStruct((value.shape[0] // cuts, value.shape[1]), value.dtype),
        in_specs=[pl.BlockSpec(memory_space=pltpu.SMEM), anywhere, [anywhere] * len(after)],
        out_specs=pl.BlockSpec(memory_space=pltpu.VMEM),
        scratch_shapes=[pltpu.SemaphoreType.DMA((halves,))],
        compiler_params=pltpu.CompilerParams(vmem_limit_bytes=VMEM_BYTES),
        cost_estimate=pl.CostEstimate(flops=0, bytes_accessed=8 * value.size // cuts, transcendentals=0),
    )(meta, value, after)


def along(value, step):
    pairs = {
        "near": [(0, 1), (1, 0), (2, 3), (3, 2)],
        "inner": [(1, 2), (2, 1)],
        "outer": [(1, 0), (2, 3)],
        "through": [(2, 1), (1, 2)],
        "last": [(1, 0), (2, 3)],
    }
    with jax.named_scope(step):
        return lax.ppermute(value, "col", pairs[step])


def on_device(a_blocks, a_index, b_blocks, b_index, c_index):
    rows = lax.axis_size("row")
    tiles = lax.axis_size("col")
    depths = lax.axis_size("depth")
    row = lax.axis_index("row")
    z = lax.axis_index("col")
    y = lax.axis_index("depth")
    x, core = row // 2, row % 2
    halves = rows // 2
    steps, slabs, size, a_width = a_blocks.shape
    per_row = a_index.shape[2]
    b_count = b_index.shape[2]
    kept = c_index.shape[2]
    slab = b_blocks.shape[0]
    meta = jnp.stack([x, core, y, z]).astype(jnp.int32)

    mates = [(r, r ^ 1) for r in range(rows)]
    across = [(r, r ^ 2) for r in range(rows)]

    b_own = b_blocks.reshape(slab * size, -1)
    b_flat = b_index.reshape(-1)
    with jax.named_scope("mate"):
        b_mate = lax.ppermute(b_own, "row", mates)
    with jax.named_scope("mate_index"):
        m_flat = lax.ppermute(b_flat, "row", mates)

    a_by = a_blocks.reshape(steps, halves, 2, depths, size, a_width)
    i_by = a_index.reshape(steps, halves, 2, depths, per_row).astype(jnp.float32)
    c_rows = c_index.reshape(-1).astype(jnp.float32)
    c_rows = jnp.pad(c_rows, (0, (INDEX_ROWS - 1) * LANES - c_rows.size)).reshape(-1, LANES)

    def a_for(ex, e):
        def pick(value):
            value = lax.dynamic_index_in_dim(value, x ^ ex, 1, keepdims=False)
            return lax.dynamic_index_in_dim(value, y ^ e, 2, keepdims=False)

        index = pick(i_by).reshape(1, -1)
        index = jnp.pad(index, ((0, 0), (0, LANES - index.shape[1])))
        return jnp.concatenate([pick(a_by).reshape(-1, LANES), index, c_rows])

    own = a_for(0, 0)
    others = [own]
    for ex in range(halves):
        for e in range(depths):
            if ex or e:
                perm = [
                    (r * depths + d, (r ^ (2 * ex)) * depths + (d ^ e))
                    for r in range(rows)
                    for d in range(depths)
                ]
                with jax.named_scope(f"spread_{ex}{e}"):
                    others.append(lax.ppermute(a_for(ex, e), ("row", "depth"), perm))
    c_across = others[depths][1 - INDEX_ROWS:].reshape(-1)[:c_index.size].astype(jnp.int32)
    with jax.named_scope("joined"):
        here = joined(others, [])
    near, inner = along(here, "near"), along(here, "inner")
    whole_table = jnp.concatenate(
        [jnp.pad(meta, (0, 4)), b_flat, m_flat, c_index.reshape(-1), c_across]
    )

    table = [[0, 1, 2, 3], [1, 0, 3, 2], [2, 2, 1, 1], [3, 3, 0, 0]]
    per_piece = depths * steps
    part_rows = own.shape[0]
    data_rows = part_rows - INDEX_ROWS
    block_rows = rows * tiles * per_piece

    x_sums, settle, pending, order = [], [], [], []
    out = None
    number = 0
    for slot in range(tiles):
        if slot == 0:
            a_sources = [[[here]]]
        elif slot == 1:
            inner = gated(inner, order)
            near = gated(near, order + [inner])
            outer, through = along(inner, "outer"), along(near, "through")
            a_sources = [[[near]]]
        elif slot == 2:
            a_sources = [[[outer], [inner]]]
            throughs = [taken(halves, depths, CUTS[3], 0, meta, through, order + [outer])]
            order = order + throughs
        else:
            lasts = [along(value, "last") for value in throughs]
            a_sources = [[[there], [here]] for there, here in zip(lasts, throughs)]
        cuts = CUTS[slot]
        count = per_piece // cuts
        near_rows = -(-count * slab // block_rows) + 2
        dims = (halves, depths, steps, tiles, kept, per_row, b_count, slab, size, near_rows)
        for cut in range(cuts):
            after = list(order)
            if depths == 2:
                after += [settle[n][6] for n in BEFORE_SUM.get(number, [])]
                after += [settle[n][7] for n in BEFORE_OTHER.get(number, [])]
            across_here = depths if len(a_sources) == 1 else depths // cuts
            with jax.named_scope(f"placed_{slot}{cut}"):
                send, keep = placed_products(
                    dims, slot, cut * count, count, across_here, whole_table, a_sources[cut % len(a_sources)], b_own, b_mate, after
                )
            order = [keep]
            if slot == 2 and cut == 0:
                throughs += [taken(halves, depths, CUTS[3], n, meta, through, order) for n in range(1, CUTS[3])]
                order = order + throughs[1:]
            with jax.named_scope(f"x_{slot}{cut}"):
                other = lax.ppermute(send, "row", across)
            x_sums.append((keep, other))
            if depths == 2:
                perm = []
                for c in range(tiles):
                    to = table[slot][c] * depths // tiles
                    perm.append((c * depths + 1 - to, c * depths + to))
                settle.append(None)
                pending.append((number, slot, cut, count, perm))
                for item in [p for p in pending if Y_WITH[p[0]] <= number]:
                    pending.remove(item)
                    n, its_slot, its_cut, its_count, its_perm = item
                    with jax.named_scope(f"sum_{its_slot}{its_cut}"):
                        total = summed(*x_sums[n], order + [settle[m][7] for m in SUM_AFTER.get(n, [])])
                    with jax.named_scope(f"y_{its_slot}{its_cut}"):
                        other = lax.ppermute(total, ("col", "depth"), its_perm)
                    settle[n] = (its_slot, its_cut * its_count, depths, steps, tiles, meta, total, other)
            number += 1

    if depths == 2:
        for one in settle:
            out = settled(*one, out)
    if depths != 2:
        full = jnp.zeros((tiles, per_piece) + x_sums[0][0].shape[1:], jnp.float32)
        at = 0
        for slot in range(tiles):
            total = lax.psum(jnp.concatenate([one + two for one, two in x_sums[at:at + CUTS[slot]]]), "depth")
            at += CUTS[slot]
            full = lax.dynamic_update_index_in_dim(full, total, slot_piece(slot, z, tiles), 0)
        full = full.reshape((tiles * per_piece,) + x_sums[0][0].shape[1:])
        share = full.shape[0] // depths
        out = lax.dynamic_slice_in_dim(full, y * share, share, 0)[:, None]
    return out


def solution(mesh):
    return jax.shard_map(
        on_device,
        mesh=mesh,
        in_specs=(
            P(("row", "col", "depth"), None, None, None),
            P(("row", "col", "depth"), None, None),
            P(("row", "depth"), "col", None, None),
            P(("row", "depth"), "col", None),
            P("row", "col", None),
        ),
        out_specs=P(("row", "depth"), "col", None, None),
        check_vma=False,
    )
```

```python
import functools

import jax
import jax.numpy as jnp
from jax import lax
from jax.experimental import pallas as pl
from jax.experimental.pallas import tpu as pltpu
from jax.sharding import PartitionSpec as P

LANES = 128
INDEX_ROWS = 8
COST = 1000000000
VMEM_BYTES = 48 * 1024 * 1024
CUTS = (1, 1, 2, 2)
Y_WITH = {0: 1, 1: 2, 2: 3, 3: 4, 4: 5, 5: 5}
BEFORE_SUM = {5: [2]}
BEFORE_OTHER = {4: [0]}
SUM_AFTER = {4: [1, 2], 5: [3]}


def slot_piece(slot, z, tiles):
    if slot == 0:
        return z
    if slot == 1:
        return jnp.bitwise_xor(z, 1)
    if slot == 2:
        return jnp.where(z < tiles // 2, 2, 1)
    return jnp.where(z < tiles // 2, 3, 0)


def placed_kernel(dims, slot, first, count, across, table, a_refs, b_own, b_mate, after, send, keep,
                  a_buf, i_wide, i_whole, i_buf, b_buf, p_hi, p_lo, a_sem, i_sem, b_sem):
    halves, depths, steps, tiles, kept, per_row, b_count, slab, size, near_rows = dims
    x, core, y, z = (table[n] for n in range(4))
    at_mine, at_mate = 8, 8 + slab * b_count
    at_kept = at_mate + slab * b_count
    data_rows = steps * 2 * size
    part_rows = data_rows + INDEX_ROWS
    wide = 2 * size
    per_piece = depths * steps
    per_tile = tiles * per_piece
    piece = slot_piece(slot, z, tiles)
    middle = jnp.logical_and(z > 0, z < tiles - 1)

    def loads(refs):
        index, copies = [], []
        which = 0
        for ref in refs:
            for part in range(ref.shape[0] // part_rows):
                index.append(
                    pltpu.make_async_copy(
                        ref.at[pl.ds(part * part_rows + data_rows, INDEX_ROWS)],
                        i_wide.at[pl.ds(which * INDEX_ROWS, INDEX_ROWS)],
                        i_sem.at[which],
                    )
                )
                copies.append(
                    pltpu.make_async_copy(
                        ref.at[pl.ds(part * part_rows, data_rows)],
                        a_buf.at[pl.ds(which * data_rows, data_rows)],
                        a_sem.at[which],
                    )
                )
                which += 1
        return index + copies

    starts, rows = [], []
    for ex in range(halves):
        block_row = (jnp.bitwise_xor(x, ex) * 2 + core) * per_tile + piece * per_piece + first
        start = jnp.clip(block_row * slab // (halves * 2 * per_tile) - 1, 0, slab - near_rows)
        band = pl.ds(pl.multiple_of(start * size, size), near_rows * size)
        rows.append(
            [
                pltpu.make_async_copy(source.at[band], b_buf.at[ex, number], b_sem.at[ex, number])
                for number, source in enumerate((b_own, b_mate))
            ]
        )
        starts.append(start)
    for ex in reversed(range(halves)):
        for copy in rows[ex]:
            copy.start()
    if len(a_refs) == 1:
        data = loads(a_refs[0])
        for copy in data:
            copy.start()
    else:
        @pl.when(middle)
        def _():
            for copy in loads(a_refs[1]):
                copy.start()

        @pl.when(jnp.logical_not(middle))
        def _():
            for copy in loads(a_refs[0]):
                copy.start()

        data = loads(a_refs[0])
    for copy in data[:halves * across]:
        copy.wait()
    data = data[halves * across:]
    i_whole[...] = i_wide[...].astype(jnp.int32)
    whole = pltpu.make_async_copy(i_whole, i_buf, i_sem.at[halves * across])
    whole.start()
    whole.wait()

    low = lax.broadcasted_iota(jnp.int32, (8, wide), 1) < size

    def place(n):
        d = (first + n) // steps
        return jnp.bitwise_xor(y, d) % across, (first + n) % steps

    def build(ex, n, high, low_part):
        e, t = place(n)
        c_at = at_kept + (ex * per_tile + piece * per_piece + first + n) * kept
        c_of = [jnp.where(low, table[c_at + 2 * k], table[c_at + 2 * k + 1]) for k in range(kept // 2)]
        for s in range(2 * per_row):
            whose = core if s < per_row else 1 - core
            row = i_buf[(ex * across + e) * INDEX_ROWS, (t * 2 + whose) * per_row + s % per_row]
            at = (at_mine if s < per_row else at_mate) + row * b_count
            cols = [table[at + b] for b in range(b_count)]
            held_at = pl.multiple_of((row - starts[ex]) * size, size)
            wanted = []
            for b in range(0, b_count, 2):
                wanted.append(jnp.where(low, cols[b], cols[b + 1]))
                wanted.append(jnp.where(low, cols[b + 1], cols[b]))
            held = []
            for g in range(size // 8):
                row = []
                for b in range(b_count // 2):
                    v = b_buf[ex, s // per_row, pl.ds(held_at + g * 8, 8), b * wide:(b + 1) * wide]
                    row += [v, pltpu.roll(v, size, 1)]
                held.append(row)
            for k in range(kept // 2):
                masks = [w == c_of[k] for w in wanted]
                for pair in range(size // 16):
                    both = []
                    for g in (2 * pair, 2 * pair + 1):
                        got = jnp.where(masks[0], held[g][0], 0.0)
                        for m in range(1, b_count):
                            got = got + jnp.where(masks[m], held[g][m], 0.0)
                        both.append(got)
                    both = jnp.concatenate(both, axis=0)
                    hi = both.astype(jnp.bfloat16)
                    lo = (both - hi.astype(jnp.float32)).astype(jnp.bfloat16)
                    rows = slice(s * size + pair * 16, s * size + (pair + 1) * 16)
                    high[rows, k * wide:(k + 1) * wide] = hi
                    low_part[rows, k * wide:(k + 1) * wide] = lo

    def multiply(ex, n, high, low_part):
        e, t = place(n)
        base = (ex * across + e) * data_rows + t * 2 * size
        a_row = jnp.concatenate(
            [
                a_buf[pl.ds(pl.multiple_of(base + core * size, size), size)],
                a_buf[pl.ds(pl.multiple_of(base + (1 - core) * size, size), size)],
            ],
            axis=1,
        )
        a_hi = a_row.astype(jnp.bfloat16)
        a_lo = (a_row - a_hi.astype(jnp.float32)).astype(jnp.bfloat16)
        both = jnp.dot(jnp.concatenate([a_hi, a_lo], axis=0), high[...], preferred_element_type=jnp.float32)
        return both[:size] + (both[size:] + jnp.dot(a_hi, low_part[...], preferred_element_type=jnp.float32))

    for ex in reversed(range(halves)):
        for copy in rows[ex]:
            copy.wait()
        if ex == halves - 1:
            for copy in data:
                copy.wait()

        def two(m, _, ex=ex):
            for u in range(2):
                build(ex, 2 * m + u, p_hi[u], p_lo[u])
            for u in range(2):
                out = multiply(ex, 2 * m + u, p_hi[u], p_lo[u])
                if ex:
                    send[2 * m + u] = out
                else:
                    keep[2 * m + u] = out
            return 0

        lax.fori_loop(0, count // 2, two, 0)


def placed_products(dims, slot, first, count, across, table, a_sources, b_own, b_mate, after):
    halves, depths, steps, tiles, kept, per_row, b_count, slab, size, near_rows = dims
    shape = jax.ShapeDtypeStruct((count, size, kept * size), jnp.float32)
    smem = pl.BlockSpec(memory_space=pltpu.SMEM)
    anywhere = pl.BlockSpec(memory_space=pl.ANY)
    hbm = pl.BlockSpec(memory_space=pltpu.HBM)
    vmem = pl.BlockSpec(memory_space=pltpu.VMEM)
    parts = halves * across
    placed_shape = pltpu.VMEM((2 * per_row * size, kept * size), jnp.bfloat16)
    return pl.pallas_call(
        functools.partial(placed_kernel, dims, slot, first, count, across),
        out_shape=(shape, shape),
        in_specs=[smem] + [jax.tree.map(lambda _: anywhere, a_sources), hbm, hbm, [anywhere] * len(after)],
        out_specs=(vmem, vmem),
        scratch_shapes=[
            pltpu.VMEM((parts * steps * 2 * size, LANES), jnp.float32),
            pltpu.VMEM((parts * INDEX_ROWS, LANES), jnp.float32),
            pltpu.VMEM((parts * INDEX_ROWS, LANES), jnp.int32),
            pltpu.SMEM((parts * INDEX_ROWS, LANES), jnp.int32),
            pltpu.VMEM((halves, 2, near_rows * size, b_own.shape[1]), jnp.float32),
            [placed_shape] * 2,
            [placed_shape] * 2,
            pltpu.SemaphoreType.DMA((parts,)),
            pltpu.SemaphoreType.DMA((parts + 1,)),
            pltpu.SemaphoreType.DMA((halves, 2)),
        ],
        compiler_params=pltpu.CompilerParams(vmem_limit_bytes=VMEM_BYTES),
        cost_estimate=pl.CostEstimate(
            flops=COST * count * halves,
            bytes_accessed=4 * (2 * count * size * kept * size + parts * steps * 2 * size * LANES),
            transcendentals=0,
        ),
    )(table, a_sources, b_own, b_mate, after)


def joined_kernel(parts, after, out, sem):
    copies = []
    at = 0
    for number, part in enumerate(parts):
        copies.append(pltpu.make_async_copy(part, out.at[pl.ds(at, part.shape[0])], sem.at[number]))
        at += part.shape[0]
    for copy in copies:
        copy.start()
    for copy in copies:
        copy.wait()


def joined(parts, after):
    anywhere = pl.BlockSpec(memory_space=pl.ANY)
    total = sum(part.shape[0] for part in parts)
    return pl.pallas_call(
        joined_kernel,
        out_shape=jax.ShapeDtypeStruct((total,) + parts[0].shape[1:], jnp.float32),
        in_specs=[[anywhere] * len(parts), [anywhere] * len(after)],
        out_specs=pl.BlockSpec(memory_space=pltpu.VMEM),
        scratch_shapes=[pltpu.SemaphoreType.DMA((len(parts),))],
        compiler_params=pltpu.CompilerParams(vmem_limit_bytes=VMEM_BYTES),
        cost_estimate=pl.CostEstimate(flops=0, bytes_accessed=8 * total * LANES, transcendentals=0),
    )(parts, after)


def settle_kernel(slot, first, depths, steps, tiles, table, total, other, *refs):
    out, held, sem = refs[-3:]
    y, z = table[2], table[3]
    piece = slot_piece(slot, z, tiles)

    @pl.when(piece * depths // tiles == y)
    def _():
        held[...] = total[...] + other[...]
        at = piece % (tiles // depths) * depths * steps + first
        copy = pltpu.make_async_copy(held, out.at[pl.ds(at, total.shape[0]), 0], sem)
        copy.start()
        copy.wait()


def settled(slot, first, depths, steps, tiles, meta, total, other, out):
    anywhere = pl.BlockSpec(memory_space=pl.ANY)
    vmem = pl.BlockSpec(memory_space=pltpu.VMEM)
    shape = jax.ShapeDtypeStruct((tiles * steps, 1) + total.shape[1:], jnp.float32)
    so_far = [] if out is None else [out]
    return pl.pallas_call(
        functools.partial(settle_kernel, slot, first, depths, steps, tiles),
        out_shape=shape,
        in_specs=[pl.BlockSpec(memory_space=pltpu.SMEM), vmem, vmem] + [anywhere] * len(so_far),
        out_specs=anywhere,
        scratch_shapes=[pltpu.VMEM(total.shape, jnp.float32), pltpu.SemaphoreType.DMA],
        input_output_aliases={3: 0} if so_far else {},
        compiler_params=pltpu.CompilerParams(vmem_limit_bytes=VMEM_BYTES),
        cost_estimate=pl.CostEstimate(flops=0, bytes_accessed=12 * total.size, transcendentals=0),
    )(meta, total, other, *so_far)


def sum_kernel(one, two, after, out):
    out[...] = one[...] + two[...]


def summed(one, two, after):
    vmem = pl.BlockSpec(memory_space=pltpu.VMEM)
    return pl.pallas_call(
        sum_kernel,
        out_shape=jax.ShapeDtypeStruct(one.shape, one.dtype),
        in_specs=[vmem, vmem, [pl.BlockSpec(memory_space=pl.ANY)] * len(after)],
        out_specs=vmem,
        compiler_params=pltpu.CompilerParams(vmem_limit_bytes=VMEM_BYTES),
        cost_estimate=pl.CostEstimate(flops=one.size, bytes_accessed=12 * one.size, transcendentals=0),
    )(one, two, after)


def taken_kernel(halves, depths, cuts, cut, meta, value, after, out, sem):
    y = meta[2]
    length = value.shape[0] // (halves * cuts)
    copies = []
    for ex in range(halves):
        at = pl.multiple_of((ex * cuts + jnp.bitwise_xor(y // (depths // cuts), cut)) * length, 8)
        copies.append(pltpu.make_async_copy(value.at[pl.ds(at, length)], out.at[pl.ds(ex * length, length)], sem.at[ex]))
    for copy in copies:
        copy.start()
    for copy in copies:
        copy.wait()


def taken(halves, depths, cuts, cut, meta, value, after):
    anywhere = pl.BlockSpec(memory_space=pl.ANY)
    return pl.pallas_call(
        functools.partial(taken_kernel, halves, depths, cuts, cut),
        out_shape=jax.ShapeDtypeStruct((value.shape[0] // cuts, value.shape[1]), value.dtype),
        in_specs=[pl.BlockSpec(memory_space=pltpu.SMEM), anywhere, [anywhere] * len(after)],
        out_specs=pl.BlockSpec(memory_space=pltpu.VMEM),
        scratch_shapes=[pltpu.SemaphoreType.DMA((halves,))],
        compiler_params=pltpu.CompilerParams(vmem_limit_bytes=VMEM_BYTES),
        cost_estimate=pl.CostEstimate(flops=0, bytes_accessed=8 * value.size // cuts, transcendentals=0),
    )(meta, value, after)


def along(value, step):
    pairs = {
        "near": [(0, 1), (1, 0), (2, 3), (3, 2)],
        "inner": [(1, 2), (2, 1)],
        "outer": [(1, 0), (2, 3)],
        "through": [(2, 1), (1, 2)],
        "last": [(1, 0), (2, 3)],
    }
    with jax.named_scope(step):
        return lax.ppermute(value, "col", pairs[step])


def on_device(a_blocks, a_index, b_blocks, b_index, c_index):
    rows = lax.axis_size("row")
    tiles = lax.axis_size("col")
    depths = lax.axis_size("depth")
    row = lax.axis_index("row")
    z = lax.axis_index("col")
    y = lax.axis_index("depth")
    x, core = row // 2, row % 2
    halves = rows // 2
    steps, slabs, size, a_width = a_blocks.shape
    per_row = a_index.shape[2]
    b_count = b_index.shape[2]
    kept = c_index.shape[2]
    slab = b_blocks.shape[0]
    meta = jnp.stack([x, core, y, z]).astype(jnp.int32)

    mates = [(r, r ^ 1) for r in range(rows)]
    across = [(r, r ^ 2) for r in range(rows)]

    b_own = b_blocks.reshape(slab * size, -1)
    b_flat = b_index.reshape(-1)
    with jax.named_scope("mate"):
        b_mate = lax.ppermute(b_own, "row", mates)
    with jax.named_scope("mate_index"):
        m_flat = lax.ppermute(b_flat, "row", mates)

    a_by = a_blocks.reshape(steps, halves, 2, depths, size, a_width)
    i_by = a_index.reshape(steps, halves, 2, depths, per_row).astype(jnp.float32)
    c_rows = c_index.reshape(-1).astype(jnp.float32)
    c_rows = jnp.pad(c_rows, (0, (INDEX_ROWS - 1) * LANES - c_rows.size)).reshape(-1, LANES)

    def a_for(ex, e):
        def pick(value):
            value = lax.dynamic_index_in_dim(value, x ^ ex, 1, keepdims=False)
            return lax.dynamic_index_in_dim(value, y ^ e, 2, keepdims=False)

        index = pick(i_by).reshape(1, -1)
        index = jnp.pad(index, ((0, 0), (0, LANES - index.shape[1])))
        return jnp.concatenate([pick(a_by).reshape(-1, LANES), index, c_rows])

    own = a_for(0, 0)
    others = []
    for ex in range(halves):
        for e in range(depths):
            if ex or e:
                perm = [
                    (r * depths + d, (r ^ (2 * ex)) * depths + (d ^ e))
                    for r in range(rows)
                    for d in range(depths)
                ]
                with jax.named_scope(f"spread_{ex}{e}"):
                    others.append(lax.ppermute(a_for(ex, e), ("row", "depth"), perm))
    c_across = others[depths - 1][1 - INDEX_ROWS:].reshape(-1)[:c_index.size].astype(jnp.int32)
    near_own, inner_own = along(own, "near"), along(own, "inner")
    with jax.named_scope("joined"):
        rest = joined(others, [near_own, inner_own])
    near_rest, inner_rest = along(rest, "near"), along(rest, "inner")
    whole_table = jnp.concatenate(
        [jnp.pad(meta, (0, 4)), b_flat, m_flat, c_index.reshape(-1), c_across]
    )

    table = [[0, 1, 2, 3], [1, 0, 3, 2], [2, 2, 1, 1], [3, 3, 0, 0]]
    per_piece = depths * steps
    part_rows = own.shape[0]
    data_rows = part_rows - INDEX_ROWS
    block_rows = rows * tiles * per_piece

    x_sums, settle, pending, order = [], [], [], []
    out = None
    number = 0
    for slot in range(tiles):
        if slot == 0:
            a_sources = [[[own, rest]]]
        elif slot == 1:
            inner = joined([inner_own, inner_rest], order)
            near = joined([near_own, near_rest], order + [inner])
            outer, through = along(inner, "outer"), along(near, "through")
            a_sources = [[[near]]]
        elif slot == 2:
            a_sources = [[[outer], [inner]]]
            throughs = [taken(halves, depths, CUTS[3], 0, meta, through, order + [outer])]
            order = order + throughs
        else:
            lasts = [along(value, "last") for value in throughs]
            a_sources = [[[there], [here]] for there, here in zip(lasts, throughs)]
        cuts = CUTS[slot]
        count = per_piece // cuts
        near_rows = -(-count * slab // block_rows) + 2
        dims = (halves, depths, steps, tiles, kept, per_row, b_count, slab, size, near_rows)
        for cut in range(cuts):
            after = list(order)
            if depths == 2:
                after += [settle[n][6] for n in BEFORE_SUM.get(number, [])]
                after += [settle[n][7] for n in BEFORE_OTHER.get(number, [])]
            across_here = depths if len(a_sources) == 1 else depths // cuts
            with jax.named_scope(f"placed_{slot}{cut}"):
                send, keep = placed_products(
                    dims, slot, cut * count, count, across_here, whole_table, a_sources[cut % len(a_sources)], b_own, b_mate, after
                )
            order = [keep]
            if slot == 2 and cut == 0:
                throughs += [taken(halves, depths, CUTS[3], n, meta, through, order) for n in range(1, CUTS[3])]
                order = order + throughs[1:]
            with jax.named_scope(f"x_{slot}{cut}"):
                other = lax.ppermute(send, "row", across)
            x_sums.append((keep, other))
            if depths == 2:
                perm = []
                for c in range(tiles):
                    to = table[slot][c] * depths // tiles
                    perm.append((c * depths + 1 - to, c * depths + to))
                settle.append(None)
                pending.append((number, slot, cut, count, perm))
                for item in [p for p in pending if Y_WITH[p[0]] <= number]:
                    pending.remove(item)
                    n, its_slot, its_cut, its_count, its_perm = item
                    with jax.named_scope(f"sum_{its_slot}{its_cut}"):
                        total = summed(*x_sums[n], order + [settle[m][7] for m in SUM_AFTER.get(n, [])])
                    with jax.named_scope(f"y_{its_slot}{its_cut}"):
                        other = lax.ppermute(total, ("col", "depth"), its_perm)
                    settle[n] = (its_slot, its_cut * its_count, depths, steps, tiles, meta, total, other)
            number += 1

    if depths == 2:
        for one in settle:
            out = settled(*one, out)
    if depths != 2:
        full = jnp.zeros((tiles, per_piece) + x_sums[0][0].shape[1:], jnp.float32)
        at = 0
        for slot in range(tiles):
            total = lax.psum(jnp.concatenate([one + two for one, two in x_sums[at:at + CUTS[slot]]]), "depth")
            at += CUTS[slot]
            full = lax.dynamic_update_index_in_dim(full, total, slot_piece(slot, z, tiles), 0)
        full = full.reshape((tiles * per_piece,) + x_sums[0][0].shape[1:])
        share = full.shape[0] // depths
        out = lax.dynamic_slice_in_dim(full, y * share, share, 0)[:, None]
    return out


def solution(mesh):
    return jax.shard_map(
        on_device,
        mesh=mesh,
        in_specs=(
            P(("row", "col", "depth"), None, None, None),
            P(("row", "col", "depth"), None, None),
            P(("row", "depth"), "col", None, None),
            P(("row", "depth"), "col", None),
            P("row", "col", None),
        ),
        out_specs=P(("row", "depth"), "col", None, None),
        check_vma=False,
    )
```
